32 devices in a mesh: tm: 4 (over x, core), height: 2 (over y), width: 4 (over z).
Axes of the slice: x: 2, y: 2, z: 4, core: 2. Of those that a mesh axis runs over, the one named last changes fastest.
Arguments:
- frames: bfloat16 [8, 8, 128, 384], P('tm', 'height', 'width'), may hold values from -6 to 6
- cache_in: bfloat16 [2, 8, 128, 384], P(None, 'height', 'width'), may hold values from -6 to 6
- kernel: bfloat16 [384, 3, 3, 3, 384], replicated, may hold values from -0.0625 to 0.0625
- conv_bias: float32 [384], replicated, may hold values from -3 to 3
- cotangent: bfloat16 [8, 8, 128, 384], P('tm', 'height', 'width'), may hold values from -6 to 6
Outputs:
- decoded: bfloat16 [8, 8, 128, 384], P('tm', 'height', 'width')
- frame_grad: bfloat16 [8, 8, 128, 384], P('tm', 'height', 'width')
- cache_grad: bfloat16 [8, 8, 128, 384], P('tm', 'height', 'width')
- kernel_grad: float32 [384, 3, 3, 3, 384], P('height')
The draws below stay inside these ranges and needn't reach their ends.
All inputs are finite; a program needn't handle non-finite values.
Results may differ from the reference program's by a relative error of at most 0.0053.
Values may be sent and summed in bfloat16 or wider, within the bound.
A program may use at most 256 MiB of HBM per device.

```python
import jax
import jax.numpy as jnp

C = 384
F_DEV = 2
FRAMES = 8
ROWS = 8
COLS = 128
N_TM = 4


def strengthened(entries, own_key, source, target, parts, factor):
    def block_of(axis_at):
        return (jnp.arange(entries.shape[axis_at]) // (entries.shape[axis_at] // parts)).reshape((-1,) + (1,) * (entries.ndim - 1 - axis_at))

    one_side = jax.random.permutation(own_key, parts)[block_of(target)]
    other_side = (block_of(target) + parts // 2) % parts
    return jnp.where((block_of(source) == one_side) | (block_of(source) == other_side), factor * entries, entries)


def levels(rng, extent, cuts, low, largest):
    factor_of = 1.0
    for dim, parts in cuts:
        heights = jax.random.uniform(jax.random.fold_in(jax.random.fold_in(rng, 6), dim), (parts,), jnp.float32, low / len(cuts), largest / len(cuts))
        factor_of = factor_of * jnp.repeat(jnp.exp(heights), extent[dim] // parts).reshape((-1,) + (1,) * (len(extent) - 1 - dim))
    return factor_of


def noise(key, dims, scale, reach, split=(), held_as=jnp.bfloat16):
    drawn = jax.random.normal(key, dims, jnp.float32) * scale
    if len(split) > 0:
        drawn = levels(key, dims, split, -0.22, 0.18) * drawn
    return jnp.clip(drawn, min=-reach, max=reach).astype(held_as)


def gaussian_with(key, dims, width, limit, cuts, heavy, dtype=jnp.bfloat16):
    drawn = width * jax.random.normal(key, dims, jnp.float32)
    if cuts:
        drawn = drawn * levels(key, dims, cuts, -0.22, 0.18)
    return jnp.clip(strengthened(drawn, jax.random.fold_in(key, 3), *heavy), -limit, limit).astype(dtype)


def setup_inputs(seed: int = 0) -> dict:
    key_of = jax.random.split(jax.random.key(seed), 6)
    frames = noise(key_of[0], (FRAMES, ROWS, COLS, C), 1.0, 6.0, ((0, 4), (1, 2), (2, 4)))
    cache_in = noise(key_of[1], (2, ROWS, COLS, C), 1.0, 6.0, ((1, 2), (2, 4)))
    kernel = noise(key_of[2], (C, 3, 3, 3, C), (27 * C) ** -0.5, 0.0625)
    conv_bias = noise(key_of[3], (C,), 0.5, 3.0, (), jnp.float32)
    cotangent = gaussian_with(key_of[4], (FRAMES, ROWS, COLS, C), 1.0, 6.0, ((0, 4), (1, 2), (2, 4)), (1, 3, 2, 2.0))
    return dict(frames=frames, cache_in=cache_in, kernel=kernel, conv_bias=conv_bias, cotangent=cotangent)


def tap_block(padded, tap_t, tap_h, tap_w, depth_count, row_count, col_count):
    block = padded[tap_t:tap_t + depth_count, tap_h:tap_h + row_count, tap_w:tap_w + col_count]
    return block.reshape(-1, block.shape[-1])


def reference(frames, cache_in, kernel, conv_bias, cotangent):
    frame_count, row_count, col_count, channels = frames.shape
    joined = jnp.concatenate([cache_in, frames], 0)
    padded = jnp.pad(joined, ((0, 0), (1, 1), (1, 1), (0, 0)))
    pre_act = jnp.zeros((frame_count * row_count * col_count, channels), jnp.float32) + conv_bias
    for tap_t in range(3):
        for tap_h in range(3):
            for tap_w in range(3):
                block = tap_block(padded, tap_t, tap_h, tap_w, frame_count, row_count, col_count)
                pre_act = pre_act + jnp.dot(block, kernel[:, tap_t, tap_h, tap_w, :].T, preferred_element_type=jnp.float32)
    sigma = jax.nn.sigmoid(pre_act)
    decoded = (pre_act * sigma).astype(jnp.bfloat16).reshape(frames.shape)
    scaled = (cotangent.reshape(-1, channels).astype(jnp.float32) * sigma * (1.0 + pre_act * (1.0 - sigma))).astype(jnp.bfloat16)
    grad_pad = jnp.pad(scaled.reshape(frames.shape), ((0, 0), (1, 1), (1, 1), (0, 0)))
    partial_value = jnp.zeros((N_TM, F_DEV + 2, row_count, col_count, channels), jnp.float32)
    for tap_t in range(3):
        contrib = jnp.zeros((frame_count * row_count * col_count, channels), jnp.float32)
        for tap_h in range(3):
            for tap_w in range(3):
                block = grad_pad[:, 2 - tap_h:2 - tap_h + row_count, 2 - tap_w:2 - tap_w + col_count].reshape(-1, channels)
                contrib = contrib + jnp.dot(block, kernel[:, tap_t, tap_h, tap_w, :], preferred_element_type=jnp.float32)
        partial_value = partial_value.at[:, tap_t:tap_t + F_DEV].add(contrib.reshape(N_TM, F_DEV, row_count, col_count, channels))
    head = partial_value[:, :2].astype(jnp.bfloat16)
    cache_grad = head.reshape(2 * N_TM, row_count, col_count, channels)
    carried = jnp.concatenate([head[1:], jnp.zeros_like(head[:1])], 0)
    tail = partial_value[:, 2:].at[:, F_DEV - 2:].add(carried.astype(jnp.float32))
    frame_grad = tail.reshape(frames.shape).astype(jnp.bfloat16)
    pieces = []
    for tap_t in range(3):
        for tap_h in range(3):
            for tap_w in range(3):
                block = tap_block(padded, tap_t, tap_h, tap_w, frame_count, row_count, col_count)
                pieces.append(jnp.dot(scaled.T, block, preferred_element_type=jnp.float32))
    kernel_grad = jnp.stack(pieces, 1).reshape(channels, 3, 3, 3, channels)
    return decoded, frame_grad, cache_grad, kernel_grad
```

```python
import functools

import jax
import jax.numpy as jnp
from jax import lax
from jax.experimental import pallas as pl
from jax.experimental.pallas import tpu as pltpu
from jax.sharding import PartitionSpec as P

VMEM_LIMIT = 48 * 1024 * 1024


def shifted(value, axis, by):
    length = lax.axis_size(axis)
    pairs = [(i, i + by) for i in range(length) if 0 <= i + by < length]
    return lax.ppermute(value, axis, pairs)


def with_halo(value, axis, dim):
    length = value.shape[dim]
    before = shifted(lax.slice_in_dim(value, length - 1, length, axis=dim), axis, 1)
    after = shifted(lax.slice_in_dim(value, 0, 1, axis=dim), axis, -1)
    return jnp.concatenate([before, value, after], axis=dim)


def column_taps(padded, columns):
    return jnp.stack([padded[:, :, c : c + columns] for c in range(3)], 0)


def full_spec(shape):
    return pl.BlockSpec(shape, lambda *_: (0,) * len(shape), pipeline_mode=pl.Buffered(1))


def forward_kernel(rows, columns, taps_ref, kernel_ref, bias_ref, cot_ref, dec_ref, sc_ref, acc):
    step = pl.program_id(0)
    tap_t, tap_h = step // 3, step % 3
    channels = acc.shape[1]
    total = None
    for c in range(3):
        block = taps_ref[c, pl.ds(tap_t, 2), pl.ds(tap_h, rows)].reshape(-1, channels)
        part = lax.dot_general(
            block, kernel_ref[c], (((1,), (1,)), ((), ())), preferred_element_type=jnp.float32
        )
        total = part if total is None else total + part

    @pl.when(step == 0)
    def _():
        acc[...] = total + bias_ref[...]

    @pl.when(step > 0)
    def _():
        acc[...] += total

    @pl.when(step == 8)
    def _():
        pre = acc[...]
        sigma = jax.nn.sigmoid(pre)
        dec_ref[...] = (pre * sigma).astype(jnp.bfloat16)
        cot = cot_ref[...].astype(jnp.float32)
        sc_ref[...] = (cot * sigma * (1.0 + pre * (1.0 - sigma))).astype(jnp.bfloat16)


def forward(taps, kernel, bias, cotangent):
    _, _, rows, columns, channels = taps.shape
    rows -= 2
    count = 2 * rows * columns
    flat = jax.ShapeDtypeStruct((count, channels), jnp.bfloat16)
    return pl.pallas_call(
        functools.partial(forward_kernel, rows, columns),
        grid=(9,),
        in_specs=[
            full_spec(taps.shape),
            pl.BlockSpec((3, channels, channels), lambda s: (s, 0, 0)),
            full_spec((1, channels)),
            full_spec((count, channels)),
        ],
        out_specs=[full_spec((count, channels))] * 2,
        out_shape=[flat, flat],
        scratch_shapes=[pltpu.VMEM((count, channels), jnp.float32)],
        compiler_params=pltpu.CompilerParams(vmem_limit_bytes=VMEM_LIMIT),
        cost_estimate=pl.CostEstimate(
            flops=54 * count * channels * channels,
            bytes_accessed=54 * channels * channels,
            transcendentals=count * channels,
        ),
        name="conv_forward",
    )(taps, kernel, bias, cotangent)


def data_kernel(rows, columns, taps_ref, kernel_ref, part_ref):
    step = pl.program_id(0)
    tap_t, tap_h = step // 3, step % 3
    count, channels = rows * columns, part_ref.shape[-1]
    total = None
    for c in range(3):
        block = taps_ref[2 - c, :, pl.ds(2 - tap_h, rows)].reshape(-1, channels)
        part = jnp.dot(block, kernel_ref[c], preferred_element_type=jnp.float32)
        total = part if total is None else total + part

    @pl.when(step == 0)
    def _():
        part_ref[...] = jnp.zeros_like(part_ref)

    part_ref[pl.ds(tap_t, 2)] += total.reshape(2, count, channels)


def data_grad(taps, kernel):
    _, _, rows, columns, channels = taps.shape
    rows -= 2
    shape = (4, rows * columns, channels)
    return pl.pallas_call(
        functools.partial(data_kernel, rows, columns),
        grid=(9,),
        in_specs=[
            full_spec(taps.shape),
            pl.BlockSpec((3, channels, channels), lambda s: (s, 0, 0)),
        ],
        out_specs=full_spec(shape),
        out_shape=jax.ShapeDtypeStruct(shape, jnp.float32),
        compiler_params=pltpu.CompilerParams(vmem_limit_bytes=VMEM_LIMIT),
        cost_estimate=pl.CostEstimate(
            flops=108 * rows * columns * channels * channels,
            bytes_accessed=54 * channels * channels,
            transcendentals=0,
        ),
        name="conv_data_grad",
    )(taps, kernel)


def weight_kernel(rows, taps_ref, scaled_ref, out_ref):
    step = pl.program_id(0)
    tap_t, tap_h = step // 3, step % 3
    channels = out_ref.shape[-1]
    for c in range(3):
        block = taps_ref[c, pl.ds(tap_t, 2), pl.ds(tap_h, rows)].reshape(-1, channels)
        part = jnp.dot(scaled_ref[...], block, preferred_element_type=jnp.float32)
        out_ref[c] = part.astype(out_ref.dtype)


def weight_grad(taps, scaled_t):
    _, _, rows, columns, channels = taps.shape
    rows -= 2
    owned = scaled_t.shape[0]
    return pl.pallas_call(
        functools.partial(weight_kernel, rows),
        grid=(9,),
        in_specs=[full_spec(taps.shape), full_spec(scaled_t.shape)],
        out_specs=pl.BlockSpec((3, owned, channels), lambda s: (s, 0, 0)),
        out_shape=jax.ShapeDtypeStruct((27, owned, channels), jnp.bfloat16),
        compiler_params=pltpu.CompilerParams(vmem_limit_bytes=VMEM_LIMIT),
        cost_estimate=pl.CostEstimate(
            flops=108 * rows * columns * owned * channels,
            bytes_accessed=54 * owned * channels,
            transcendentals=0,
        ),
        name="conv_weight_grad",
    )(taps, scaled_t)


def body(frames, cache_in, kernel, conv_bias, cotangent):
    _, rows, columns, channels = frames.shape
    heights = lax.axis_size("height")
    place = lax.axis_index("height")
    taps_kernel = kernel.transpose(1, 2, 3, 0, 4).reshape(27, channels, channels)

    earlier = shifted(frames, "tm", 1)
    earlier = jnp.where(lax.axis_index("tm") == 0, cache_in, earlier)
    stacked = jnp.concatenate([earlier, frames], 0)
    extended = with_halo(with_halo(stacked, "height", 1), "width", 2)
    taps = column_taps(extended, columns)
    decoded, scaled = forward(
        taps, taps_kernel, conv_bias.reshape(1, channels), cotangent.reshape(-1, channels)
    )
    scaled4 = scaled.reshape(frames.shape)

    if heights == 2:
        half = channels // 2
        inner = extended[:, 1 : rows + 1]
        swap = [(0, 1), (1, 0)]
        other = lax.ppermute(inner, "height", swap)
        edge = jnp.zeros((4, 1) + inner.shape[2:], inner.dtype)
        both = jnp.where(
            place == 0,
            jnp.concatenate([edge, inner, other, edge], 1),
            jnp.concatenate([edge, other, inner, edge], 1),
        )
        all_taps = column_taps(both, columns)
        parts = scaled4[..., :half], scaled4[..., half:]
        mine = jnp.where(place == 0, parts[0], parts[1])
        theirs = jnp.where(place == 0, parts[1], parts[0])
        got = lax.ppermute(theirs, "height", swap)
        joint = jnp.where(
            place == 0, jnp.concatenate([mine, got], 1), jnp.concatenate([got, mine], 1)
        )
        owned = weight_grad(all_taps, joint.reshape(-1, half).T)
    else:
        owned = weight_grad(taps, scaled.T)
        owned = lax.psum_scatter(owned, "height", scatter_dimension=1, tiled=True)
    summed = lax.psum(owned, ("tm", "width")).astype(jnp.float32)
    kernel_grad = summed.reshape(3, 3, 3, -1, channels).transpose(3, 0, 1, 2, 4)

    grad_taps = column_taps(with_halo(with_halo(scaled4, "height", 1), "width", 2), columns)
    partial = data_grad(grad_taps, taps_kernel).reshape(4, rows, columns, channels)
    cache_grad = partial[:2].astype(jnp.bfloat16)
    carried = shifted(cache_grad, "tm", -1)
    frame_grad = (partial[2:] + carried.astype(jnp.float32)).astype(jnp.bfloat16)
    return decoded.reshape(frames.shape), frame_grad, cache_grad, kernel_grad


def solution(mesh):
    split = P("tm", "height", "width", None)
    in_specs = (split, P(None, "height", "width", None), P(), P(), split)
    out_specs = (split, split, split, P("height", None, None, None, None))
    return jax.shard_map(body, mesh=mesh, in_specs=in_specs, out_specs=out_specs, check_vma=False)
```

```python
import functools

import jax
import jax.numpy as jnp
from jax import lax
from jax.experimental import pallas as pl
from jax.experimental.pallas import tpu as pltpu
from jax.sharding import PartitionSpec as P

VMEM_LIMIT = 48 * 1024 * 1024


def shifted(value, axis, by):
    length = lax.axis_size(axis)
    pairs = [(i, i + by) for i in range(length) if 0 <= i + by < length]
    return lax.ppermute(value, axis, pairs)


def with_halo(value, axis, dim):
    length = value.shape[dim]
    before = shifted(lax.slice_in_dim(value, length - 1, length, axis=dim), axis, 1)
    after = shifted(lax.slice_in_dim(value, 0, 1, axis=dim), axis, -1)
    return jnp.concatenate([before, value, after], axis=dim)


def column_taps(padded, columns):
    return jnp.stack([padded[:, :, c : c + columns] for c in range(3)], 0)


def full_spec(shape):
    return pl.BlockSpec(shape, lambda *_: (0,) * len(shape), pipeline_mode=pl.Buffered(1))


def first_row(paired, rows):
    return lax.axis_index("height") * rows if paired else 0


def forward_kernel(rows, paired, taps_ref, kernel_ref, bias_ref, cot_ref, dec_ref, sc_ref, acc):
    step = pl.program_id(0)
    tap_t, tap_h = step // 3, step % 3
    channels = acc.shape[1]
    start = first_row(paired, rows)
    total = None
    for c in range(3):
        block = taps_ref[c, pl.ds(tap_t, 2), pl.ds(start + tap_h, rows)].reshape(-1, channels)
        part = lax.dot_general(
            block, kernel_ref[c], (((1,), (1,)), ((), ())), preferred_element_type=jnp.float32
        )
        total = part if total is None else total + part

    @pl.when(step == 0)
    def _():
        acc[...] = total + bias_ref[...]

    @pl.when(step > 0)
    def _():
        acc[...] += total

    @pl.when(step == 8)
    def _():
        pre = acc[...]
        sigma = jax.nn.sigmoid(pre)
        dec_ref[...] = (pre * sigma).astype(jnp.bfloat16)
        cot = cot_ref[...].astype(jnp.float32)
        sc_ref[...] = (cot * sigma * (1.0 + pre * (1.0 - sigma))).astype(jnp.bfloat16)


def forward(taps, kernel, bias, cotangent, rows, paired):
    _, _, _, columns, channels = taps.shape
    count = 2 * rows * columns
    flat = jax.ShapeDtypeStruct((count, channels), jnp.bfloat16)
    return pl.pallas_call(
        functools.partial(forward_kernel, rows, paired),
        grid=(9,),
        in_specs=[
            full_spec(taps.shape),
            pl.BlockSpec((3, channels, channels), lambda s: (s, 0, 0)),
            full_spec((1, channels)),
            full_spec((count, channels)),
        ],
        out_specs=[full_spec((count, channels))] * 2,
        out_shape=[flat, flat],
        scratch_shapes=[pltpu.VMEM((count, channels), jnp.float32)],
        compiler_params=pltpu.CompilerParams(vmem_limit_bytes=VMEM_LIMIT),
        cost_estimate=pl.CostEstimate(
            flops=54 * count * channels * channels,
            bytes_accessed=54 * channels * channels,
            transcendentals=count * channels,
        ),
        name="conv_forward",
    )(taps, kernel, bias, cotangent)


def data_kernel(rows, columns, paired, taps_ref, kernel_ref, part_ref):
    step = pl.program_id(0)
    tap_t, tap_h = step // 3, step % 3
    count, channels = rows * columns, part_ref.shape[-1]
    start = first_row(paired, rows)
    total = None
    for c in range(3):
        block = taps_ref[2 - c, :, pl.ds(start + 2 - tap_h, rows)].reshape(-1, channels)
        part = jnp.dot(block, kernel_ref[c], preferred_element_type=jnp.float32)
        total = part if total is None else total + part

    @pl.when(step == 0)
    def _():
        part_ref[...] = jnp.zeros_like(part_ref)

    part_ref[pl.ds(tap_t, 2)] += total.reshape(2, count, channels)


def data_grad(taps, kernel, rows, paired):
    _, _, _, columns, channels = taps.shape
    shape = (4, rows * columns, channels)
    return pl.pallas_call(
        functools.partial(data_kernel, rows, columns, paired),
        grid=(9,),
        in_specs=[
            full_spec(taps.shape),
            pl.BlockSpec((3, channels, channels), lambda s: (s, 0, 0)),
        ],
        out_specs=full_spec(shape),
        out_shape=jax.ShapeDtypeStruct(shape, jnp.float32),
        compiler_params=pltpu.CompilerParams(vmem_limit_bytes=VMEM_LIMIT),
        cost_estimate=pl.CostEstimate(
            flops=108 * rows * columns * channels * channels,
            bytes_accessed=54 * channels * channels,
            transcendentals=0,
        ),
        name="conv_data_grad",
    )(taps, kernel)


def weight_kernel(rows, taps_ref, scaled_ref, out_ref):
    step = pl.program_id(0)
    tap_t, tap_h = step // 3, step % 3
    channels = out_ref.shape[-1]
    for c in range(3):
        block = taps_ref[c, pl.ds(tap_t, 2), pl.ds(tap_h, rows)].reshape(-1, channels)
        part = jnp.dot(scaled_ref[...], block, preferred_element_type=jnp.float32)
        out_ref[c] = part.astype(out_ref.dtype)


def weight_grad(taps, scaled_t):
    _, _, rows, columns, channels = taps.shape
    rows -= 2
    owned = scaled_t.shape[0]
    return pl.pallas_call(
        functools.partial(weight_kernel, rows),
        grid=(9,),
        in_specs=[full_spec(taps.shape), full_spec(scaled_t.shape)],
        out_specs=pl.BlockSpec((3, owned, channels), lambda s: (s, 0, 0)),
        out_shape=jax.ShapeDtypeStruct((27, owned, channels), jnp.bfloat16),
        compiler_params=pltpu.CompilerParams(vmem_limit_bytes=VMEM_LIMIT),
        cost_estimate=pl.CostEstimate(
            flops=108 * rows * columns * owned * channels,
            bytes_accessed=54 * owned * channels,
            transcendentals=0,
        ),
        name="conv_weight_grad",
    )(taps, scaled_t)


def exchange_kernel(depth, *refs):
    sources, edges = refs[:depth], refs[depth : 2 * depth]
    main_ref, edge_ref, send_sem, recv_sem = refs[2 * depth :]
    mesh_id = pl.DeviceIdType.MESH
    k, h, w = (lax.axis_index(axis) for axis in ("tm", "height", "width"))
    times, widths = lax.axis_size("tm"), lax.axis_size("width")
    left, right = lax.rem(w + widths - 1, widths), lax.rem(w + 1, widths)

    barrier = pltpu.get_barrier_semaphore()
    count = 0
    for slot in range(2 * depth):
        dk, dh = slot // 2, slot % 2
        sender = lax.rem(k + times - dk, times), (1 - h if dh else h)
        for column in (left, right) + ((w,) if slot else ()):
            pl.semaphore_signal(
                barrier, inc=1, device_id=sender + (column,), device_id_type=mesh_id
            )
            count += 1
    pl.semaphore_wait(barrier, count)

    copies = []
    for slot in range(2 * depth):
        dk, dh = slot // 2, slot % 2
        target = lax.rem(k + dk, times), (1 - h if dh else h)
        plan = [(edges[dk].at[0], edge_ref.at[slot, 0], left)]
        plan.append((edges[dk].at[1], edge_ref.at[slot, 1], right))
        if slot:
            plan.append((sources[dk], main_ref.at[slot - 1], w))
        for source, place, column in plan:
            index = len(copies)
            copy = pltpu.make_async_remote_copy(
                src_ref=source,
                dst_ref=place,
                send_sem=send_sem.at[index],
                recv_sem=recv_sem.at[index],
                device_id=target + (column,),
                device_id_type=mesh_id,
            )
            copy.start()
            copies.append(copy)
    for copy in copies:
        copy.wait()


def exchange(sources, collective_id):
    depth = len(sources)
    shape = sources[0].shape
    channels = shape[-1]
    rim = shape[0] * shape[1]
    padded = -(-rim // 16) * 16

    def columns_of(value):
        ends = jnp.stack([value[:, :, 0], value[:, :, -1]], 0).reshape(2, rim, channels)
        return jnp.pad(ends, ((0, 0), (0, padded - rim), (0, 0)))

    edges = [columns_of(value) for value in sources]
    copies = 6 * depth - 1
    vmem = pl.BlockSpec(memory_space=pltpu.VMEM)
    main, ends = pl.pallas_call(
        functools.partial(exchange_kernel, depth),
        in_specs=[vmem] * (2 * depth),
        out_specs=[vmem] * 2,
        out_shape=[
            jax.ShapeDtypeStruct((2 * depth - 1,) + shape, jnp.bfloat16),
            jax.ShapeDtypeStruct((2 * depth, 2, padded, channels), jnp.bfloat16),
        ],
        scratch_shapes=[pltpu.SemaphoreType.DMA((copies,)), pltpu.SemaphoreType.DMA((copies,))],
        compiler_params=pltpu.CompilerParams(collective_id=collective_id, has_side_effects=True),
        name="exchange_%d" % depth,
    )(*sources, *edges)
    ends = ends[:, :, :rim].reshape(2 * depth, 2, shape[0], shape[1], 1, channels)
    return main, ends


def join_rows(mine, other, ends_mine, ends_other):
    place, column = lax.axis_index("height"), lax.axis_index("width")
    last = lax.axis_size("width") - 1

    def wide(value, ends):
        before = jnp.where(column == 0, jnp.zeros_like(ends[1]), ends[1])
        after = jnp.where(column == last, jnp.zeros_like(ends[0]), ends[0])
        return jnp.concatenate([before, value, after], 2)

    mine, other = wide(mine, ends_mine), wide(other, ends_other)
    edge = jnp.zeros_like(mine[:, :1])
    return jnp.where(
        place == 0,
        jnp.concatenate([edge, mine, other, edge], 1),
        jnp.concatenate([edge, other, mine, edge], 1),
    )


def reduce_weights(owned):
    return lax.psum(owned, ("tm", "width")).astype(jnp.float32)


def paired_rows(frames, cache_in, kernel, bias, cotangent):
    rows, columns, channels = frames.shape[1:]
    place = lax.axis_index("height")
    is_last = lax.axis_index("tm") == lax.axis_size("tm") - 1
    onward = jnp.where(is_last, cache_in, frames)
    main, ends = exchange([frames, onward], 0)
    both = join_rows(
        jnp.concatenate([main[1], frames], 0),
        jnp.concatenate([main[2], main[0]], 0),
        jnp.concatenate([ends[2], ends[0]], 1),
        jnp.concatenate([ends[3], ends[1]], 1),
    )
    taps = column_taps(both, columns)
    decoded, scaled = forward(taps, kernel, bias, cotangent, rows, True)

    mine = scaled.reshape(frames.shape)
    main, ends = exchange([mine], 1)
    other = main[0]
    half = channels // 2
    upper, lower = jnp.where(place == 0, mine, other), jnp.where(place == 0, other, mine)
    joint = jnp.concatenate([upper, lower], 1).reshape(-1, channels)
    joint = jnp.where(place == 0, joint[:, :half], joint[:, half:])
    summed = reduce_weights(weight_grad(taps, joint.T))
    grad_taps = column_taps(join_rows(mine, other, ends[0], ends[1]), columns)
    return decoded, summed, data_grad(grad_taps, kernel, rows, True)


def single_rows(frames, cache_in, kernel, bias, cotangent):
    rows, columns, _ = frames.shape[1:]
    earlier = shifted(frames, "tm", 1)
    earlier = jnp.where(lax.axis_index("tm") == 0, cache_in, earlier)
    stacked = jnp.concatenate([earlier, frames], 0)
    taps = column_taps(with_halo(with_halo(stacked, "height", 1), "width", 2), columns)
    decoded, scaled = forward(taps, kernel, bias, cotangent, rows, False)
    owned = lax.psum_scatter(
        weight_grad(taps, scaled.T), "height", scatter_dimension=1, tiled=True
    )
    scaled4 = scaled.reshape(frames.shape)
    grad_taps = column_taps(with_halo(with_halo(scaled4, "height", 1), "width", 2), columns)
    return decoded, reduce_weights(owned), data_grad(grad_taps, kernel, rows, False)


def body(frames, cache_in, kernel, conv_bias, cotangent):
    _, rows, columns, channels = frames.shape
    taps_kernel = kernel.transpose(1, 2, 3, 0, 4).reshape(27, channels, channels)
    run = paired_rows if lax.axis_size("height") == 2 else single_rows
    decoded, summed, partial = run(
        frames,
        cache_in,
        taps_kernel,
        conv_bias.reshape(1, channels),
        cotangent.reshape(-1, channels),
    )
    kernel_grad = summed.reshape(3, 3, 3, -1, channels).transpose(3, 0, 1, 2, 4)
    partial = partial.reshape(4, rows, columns, channels)
    cache_grad = partial[:2].astype(jnp.bfloat16)
    carried = shifted(cache_grad, "tm", -1)
    frame_grad = (partial[2:] + carried.astype(jnp.float32)).astype(jnp.bfloat16)
    return decoded.reshape(frames.shape), frame_grad, cache_grad, kernel_grad


def solution(mesh):
    split = P("tm", "height", "width", None)
    in_specs = (split, P(None, "height", "width", None), P(), P(), split)
    out_specs = (split, split, split, P("height", None, None, None, None))
    return jax.shard_map(body, mesh=mesh, in_specs=in_specs, out_specs=out_specs, check_vma=False)
```

```python
import functools

import jax
import jax.numpy as jnp
from jax import lax
from jax.experimental import pallas as pl
from jax.experimental.pallas import tpu as pltpu
from jax.sharding import PartitionSpec as P

VMEM_LIMIT = 48 * 1024 * 1024
CHUNKS = 3


def shifted(value, axis, by):
    length = lax.axis_size(axis)
    pairs = [(i, i + by) for i in range(length) if 0 <= i + by < length]
    return lax.ppermute(value, axis, pairs)


def with_halo(value, axis, dim):
    length = value.shape[dim]
    before = shifted(lax.slice_in_dim(value, length - 1, length, axis=dim), axis, 1)
    after = shifted(lax.slice_in_dim(value, 0, 1, axis=dim), axis, -1)
    return jnp.concatenate([before, value, after], axis=dim)


def column_taps(padded, columns):
    return jnp.stack([padded[:, :, c : c + columns] for c in range(3)], 0)


def full_spec(shape):
    return pl.BlockSpec(shape, lambda *_: (0,) * len(shape), pipeline_mode=pl.Buffered(1))


def first_row(paired, rows):
    return lax.axis_index("height") * rows if paired else 0


def forward_kernel(rows, paired, taps_ref, kernel_ref, bias_ref, cot_ref, dec_ref, sc_ref, acc):
    step = pl.program_id(0)
    tap_t, tap_h = step // 3, step % 3
    channels = acc.shape[1]
    start = first_row(paired, rows)
    total = None
    for c in range(3):
        block = taps_ref[c, pl.ds(tap_t, 2), pl.ds(start + tap_h, rows)].reshape(-1, channels)
        part = lax.dot_general(
            block, kernel_ref[c], (((1,), (1,)), ((), ())), preferred_element_type=jnp.float32
        )
        total = part if total is None else total + part

    @pl.when(step == 0)
    def _():
        acc[...] = total + bias_ref[...]

    @pl.when(step > 0)
    def _():
        acc[...] += total

    @pl.when(step == 8)
    def _():
        pre = acc[...]
        sigma = jax.nn.sigmoid(pre)
        dec_ref[...] = (pre * sigma).astype(jnp.bfloat16)
        cot = cot_ref[...].astype(jnp.float32)
        sc_ref[...] = (cot * sigma * (1.0 + pre * (1.0 - sigma))).astype(jnp.bfloat16)


def forward(taps, kernel, bias, cotangent, rows, paired):
    _, _, _, columns, channels = taps.shape
    count = 2 * rows * columns
    flat = jax.ShapeDtypeStruct((count, channels), jnp.bfloat16)
    return pl.pallas_call(
        functools.partial(forward_kernel, rows, paired),
        grid=(9,),
        in_specs=[
            full_spec(taps.shape),
            pl.BlockSpec((3, channels, channels), lambda s: (s, 0, 0)),
            full_spec((1, channels)),
            full_spec((count, channels)),
        ],
        out_specs=[full_spec((count, channels))] * 2,
        out_shape=[flat, flat],
        scratch_shapes=[pltpu.VMEM((count, channels), jnp.float32)],
        compiler_params=pltpu.CompilerParams(vmem_limit_bytes=VMEM_LIMIT),
        cost_estimate=pl.CostEstimate(
            flops=54 * count * channels * channels,
            bytes_accessed=54 * channels * channels,
            transcendentals=count * channels,
        ),
        name="conv_forward",
    )(taps, kernel, bias, cotangent)


def data_kernel(rows, columns, paired, taps_ref, kernel_ref, part_ref):
    step = pl.program_id(0)
    tap_t, tap_h = step // 3, step % 3
    count, channels = rows * columns, part_ref.shape[-1]
    start = first_row(paired, rows)
    total = None
    for c in range(3):
        block = taps_ref[2 - c, :, pl.ds(start + 2 - tap_h, rows)].reshape(-1, channels)
        part = jnp.dot(block, kernel_ref[c], preferred_element_type=jnp.float32)
        total = part if total is None else total + part

    @pl.when(step == 0)
    def _():
        part_ref[...] = jnp.zeros_like(part_ref)

    part_ref[pl.ds(tap_t, 2)] += total.reshape(2, count, channels)


def data_grad(taps, kernel, rows, paired):
    _, _, _, columns, channels = taps.shape
    shape = (4, rows * columns, channels)
    return pl.pallas_call(
        functools.partial(data_kernel, rows, columns, paired),
        grid=(9,),
        in_specs=[
            full_spec(taps.shape),
            pl.BlockSpec((3, channels, channels), lambda s: (s, 0, 0)),
        ],
        out_specs=full_spec(shape),
        out_shape=jax.ShapeDtypeStruct(shape, jnp.float32),
        compiler_params=pltpu.CompilerParams(vmem_limit_bytes=VMEM_LIMIT),
        cost_estimate=pl.CostEstimate(
            flops=108 * rows * columns * channels * channels,
            bytes_accessed=54 * channels * channels,
            transcendentals=0,
        ),
        name="conv_data_grad",
    )(taps, kernel)


def weight_kernel(rows, taps_ref, scaled_ref, out_ref):
    step = pl.program_id(0)
    tap_t, tap_h = step // 3, step % 3
    channels = out_ref.shape[-1]
    for c in range(3):
        block = taps_ref[c, pl.ds(tap_t, 2), pl.ds(tap_h, rows)].reshape(-1, channels)
        part = jnp.dot(scaled_ref[...], block, preferred_element_type=jnp.float32)
        out_ref[c] = part.astype(out_ref.dtype)


def weight_grad(taps, scaled_t):
    _, _, rows, columns, channels = taps.shape
    rows -= 2
    owned = scaled_t.shape[0]
    return pl.pallas_call(
        functools.partial(weight_kernel, rows),
        grid=(9,),
        in_specs=[full_spec(taps.shape), full_spec(scaled_t.shape)],
        out_specs=pl.BlockSpec((3, owned, channels), lambda s: (s, 0, 0)),
        out_shape=jax.ShapeDtypeStruct((28, owned, channels), jnp.bfloat16),
        compiler_params=pltpu.CompilerParams(vmem_limit_bytes=VMEM_LIMIT),
        cost_estimate=pl.CostEstimate(
            flops=108 * rows * columns * owned * channels,
            bytes_accessed=54 * owned * channels,
            transcendentals=0,
        ),
        name="conv_weight_grad",
    )(taps, scaled_t)


def exchange_kernel(depth, *refs):
    sources, edges = refs[:depth], refs[depth : 2 * depth]
    main_ref, edge_ref, send_sem, recv_sem = refs[2 * depth :]
    mesh_id = pl.DeviceIdType.MESH
    k, h, w = (lax.axis_index(axis) for axis in ("tm", "height", "width"))
    times, widths = lax.axis_size("tm"), lax.axis_size("width")
    left, right = lax.rem(w + widths - 1, widths), lax.rem(w + 1, widths)

    barrier = pltpu.get_barrier_semaphore()
    count = 0
    for slot in range(2 * depth):
        dk, dh = slot // 2, slot % 2
        sender = lax.rem(k + times - dk, times), (1 - h if dh else h)
        for column in (left, right) + ((w,) if slot else ()):
            pl.semaphore_signal(
                barrier, inc=1, device_id=sender + (column,), device_id_type=mesh_id
            )
            count += 1
    pl.semaphore_wait(barrier, count)

    copies = []
    for slot in range(2 * depth):
        dk, dh = slot // 2, slot % 2
        target = lax.rem(k + dk, times), (1 - h if dh else h)
        plan = [(edges[dk].at[0], edge_ref.at[slot, 0], left)]
        plan.append((edges[dk].at[1], edge_ref.at[slot, 1], right))
        if slot:
            plan.append((sources[dk], main_ref.at[slot - 1], w))
        for source, place, column in plan:
            index = len(copies)
            copy = pltpu.make_async_remote_copy(
                src_ref=source,
                dst_ref=place,
                send_sem=send_sem.at[index],
                recv_sem=recv_sem.at[index],
                device_id=target + (column,),
                device_id_type=mesh_id,
            )
            copy.start()
            copies.append(copy)
    for copy in copies:
        copy.wait()


def exchange(sources, collective_id):
    depth = len(sources)
    shape = sources[0].shape
    channels = shape[-1]
    rim = shape[0] * shape[1]
    padded = -(-rim // 16) * 16

    def columns_of(value):
        ends = jnp.stack([value[:, :, 0], value[:, :, -1]], 0).reshape(2, rim, channels)
        return jnp.pad(ends, ((0, 0), (0, padded - rim), (0, 0)))

    edges = [columns_of(value) for value in sources]
    copies = 6 * depth - 1
    vmem = pl.BlockSpec(memory_space=pltpu.VMEM)
    main, ends = pl.pallas_call(
        functools.partial(exchange_kernel, depth),
        in_specs=[vmem] * (2 * depth),
        out_specs=[vmem] * 2,
        out_shape=[
            jax.ShapeDtypeStruct((2 * depth - 1,) + shape, jnp.bfloat16),
            jax.ShapeDtypeStruct((2 * depth, 2, padded, channels), jnp.bfloat16),
        ],
        scratch_shapes=[pltpu.SemaphoreType.DMA((copies,)), pltpu.SemaphoreType.DMA((copies,))],
        compiler_params=pltpu.CompilerParams(collective_id=collective_id, has_side_effects=True),
        name="exchange_%d" % depth,
    )(*sources, *edges)
    ends = ends[:, :, :rim].reshape(2 * depth, 2, shape[0], shape[1], 1, channels)
    return main, ends


def join_rows(mine, other, ends_mine, ends_other):
    place, column = lax.axis_index("height"), lax.axis_index("width")
    last = lax.axis_size("width") - 1

    def wide(value, ends):
        before = jnp.where(column == 0, jnp.zeros_like(ends[1]), ends[1])
        after = jnp.where(column == last, jnp.zeros_like(ends[0]), ends[0])
        return jnp.concatenate([before, value, after], 2)

    mine, other = wide(mine, ends_mine), wide(other, ends_other)
    edge = jnp.zeros_like(mine[:, :1])
    return jnp.where(
        place == 0,
        jnp.concatenate([edge, mine, other, edge], 1),
        jnp.concatenate([edge, other, mine, edge], 1),
    )


def sum_kernel(widths, in_ref, out_ref, got1, sent2, got2, sent3, got3, whole, send_sem, recv_sem):
    size = in_ref.shape[0] // CHUNKS
    half, quarter = size // 2, size // 4
    piece = quarter // widths
    mesh_id = pl.DeviceIdType.MESH
    k, h, w = (lax.axis_index(axis) for axis in ("tm", "height", "width"))
    core, chip = lax.rem(k, 2), k // 2
    core_mate = (k + 1 - 2 * core, h, w)
    chip_mate = (lax.rem(k + 2, 4), h, w)
    line = [(k, h, lax.rem(w + d, widths)) for d in range(1, widths)]
    f32, bf16 = jnp.float32, jnp.bfloat16

    barrier = pltpu.get_barrier_semaphore()
    for mate in [core_mate, chip_mate] + line:
        pl.semaphore_signal(barrier, inc=1, device_id=mate, device_id_type=mesh_id)
    pl.semaphore_wait(barrier, 1 + widths)

    def rows(start, count):
        return pl.ds(pl.multiple_of(start, 16), count)

    used = []

    def send(source, place, mate):
        index = len(used)
        used.append(index)
        copy = pltpu.make_async_remote_copy(
            src_ref=source,
            dst_ref=place,
            send_sem=send_sem.at[index],
            recv_sem=recv_sem.at[index],
            device_id=mate,
            device_id_type=mesh_id,
        )
        copy.start()
        return copy

    base = [c * size for c in range(CHUNKS)]
    own_half = [b + core * half for b in base]
    own_quarter = [b + chip * quarter for b in own_half]
    own_piece = [b + w * piece for b in own_quarter]

    first = [
        send(in_ref.at[rows(base[c] + (1 - core) * half, half)], got1.at[c], core_mate)
        for c in range(CHUNKS)
    ]
    second, third, fourth, fifth, sixth = [], [], [], [], []
    for c in range(CHUNKS):
        first[c].wait()
        away = (1 - chip) * quarter
        mine = in_ref[rows(own_half[c] + away, quarter)].astype(f32)
        sent2[c] = (mine + got1[c, rows(away, quarter)].astype(f32)).astype(bf16)
        second.append(send(sent2.at[c], got2.at[c], chip_mate))
    for c in range(CHUNKS):
        second[c].wait()
        mine = in_ref[rows(own_quarter[c], quarter)].astype(f32)
        mine = mine + got1[c, rows(chip * quarter, quarter)].astype(f32)
        sent3[c] = (mine + got2[c].astype(f32)).astype(bf16)
        third.append(
            [
                send(sent3.at[c, rows(mate[2] * piece, piece)], got3.at[c, d], mate)
                for d, mate in enumerate(line)
            ]
        )
    for c in range(CHUNKS):
        total = in_ref[rows(own_piece[c], piece)].astype(f32)
        total = total + got1[c, rows(chip * quarter + w * piece, piece)].astype(f32)
        total = total + got2[c, rows(w * piece, piece)].astype(f32)
        for d, copy in enumerate(third[c]):
            copy.wait()
            total = total + got3[c, d].astype(f32)
        whole[rows(own_piece[c], piece)] = total.astype(bf16)
        place = whole.at[rows(own_piece[c], piece)]
        fourth.append([send(place, place, mate) for mate in line])
    for c in range(CHUNKS):
        for copy in fourth[c]:
            copy.wait()
        place = whole.at[rows(own_quarter[c], quarter)]
        fifth.append(send(place, place, chip_mate))
    for c in range(CHUNKS):
        fifth[c].wait()
        place = whole.at[rows(own_half[c], half)]
        sixth.append(send(place, place, core_mate))
    for c in range(CHUNKS):
        sixth[c].wait()
        stop = min(base[c] + size, out_ref.shape[0])
        out_ref[base[c] : stop] = whole[base[c] : stop].astype(f32)


def sum_blocks(local, valid):
    total, channels = local.shape
    widths = lax.axis_size("width")
    size = total // CHUNKS
    half, quarter = size // 2, size // 4
    copies = CHUNKS * (4 + 2 * (widths - 1))
    bf16 = jnp.bfloat16
    vmem = pl.BlockSpec(memory_space=pltpu.VMEM)
    return pl.pallas_call(
        functools.partial(sum_kernel, widths),
        in_specs=[vmem],
        out_specs=vmem,
        out_shape=jax.ShapeDtypeStruct((valid, channels), jnp.float32),
        scratch_shapes=[
            pltpu.VMEM((CHUNKS, half, channels), bf16),
            pltpu.VMEM((CHUNKS, quarter, channels), bf16),
            pltpu.VMEM((CHUNKS, quarter, channels), bf16),
            pltpu.VMEM((CHUNKS, quarter, channels), bf16),
            pltpu.VMEM((CHUNKS, widths - 1, quarter // widths, channels), bf16),
            pltpu.VMEM((total, channels), bf16),
            pltpu.SemaphoreType.DMA((copies,)),
            pltpu.SemaphoreType.DMA((copies,)),
        ],
        compiler_params=pltpu.CompilerParams(
            collective_id=2, has_side_effects=True, vmem_limit_bytes=VMEM_LIMIT
        ),
        name="sum_blocks",
    )(local)


def reduce_weights(owned):
    return lax.psum(owned, ("tm", "width")).astype(jnp.float32)


def paired_rows(frames, cache_in, kernel, bias, cotangent):
    rows, columns, channels = frames.shape[1:]
    place = lax.axis_index("height")
    is_last = lax.axis_index("tm") == lax.axis_size("tm") - 1
    onward = jnp.where(is_last, cache_in, frames)
    main, ends = exchange([frames, onward], 0)
    both = join_rows(
        jnp.concatenate([main[1], frames], 0),
        jnp.concatenate([main[2], main[0]], 0),
        jnp.concatenate([ends[2], ends[0]], 1),
        jnp.concatenate([ends[3], ends[1]], 1),
    )
    taps = column_taps(both, columns)
    decoded, scaled = forward(taps, kernel, bias, cotangent, rows, True)

    mine = scaled.reshape(frames.shape)
    main, ends = exchange([mine], 1)
    other = main[0]
    half = channels // 2
    upper, lower = jnp.where(place == 0, mine, other), jnp.where(place == 0, other, mine)
    joint = jnp.concatenate([upper, lower], 1).reshape(-1, channels)
    joint = jnp.where(place == 0, joint[:, :half], joint[:, half:])
    local = weight_grad(taps, joint.T)
    unit = 16 * 4 * lax.axis_size("width") * CHUNKS
    if lax.axis_size("tm") == 4 and 28 * half % unit == 0:
        summed = sum_blocks(local.reshape(28 * half, channels), 27 * half)
    else:
        summed = reduce_weights(local[:27])
    grad_taps = column_taps(join_rows(mine, other, ends[0], ends[1]), columns)
    return decoded, summed, data_grad(grad_taps, kernel, rows, True)


def single_rows(frames, cache_in, kernel, bias, cotangent):
    rows, columns, _ = frames.shape[1:]
    earlier = shifted(frames, "tm", 1)
    earlier = jnp.where(lax.axis_index("tm") == 0, cache_in, earlier)
    stacked = jnp.concatenate([earlier, frames], 0)
    taps = column_taps(with_halo(with_halo(stacked, "height", 1), "width", 2), columns)
    decoded, scaled = forward(taps, kernel, bias, cotangent, rows, False)
    owned = lax.psum_scatter(
        weight_grad(taps, scaled.T)[:27], "height", scatter_dimension=1, tiled=True
    )
    scaled4 = scaled.reshape(frames.shape)
    grad_taps = column_taps(with_halo(with_halo(scaled4, "height", 1), "width", 2), columns)
    return decoded, reduce_weights(owned), data_grad(grad_taps, kernel, rows, False)


def body(frames, cache_in, kernel, conv_bias, cotangent):
    _, rows, columns, channels = frames.shape
    taps_kernel = kernel.transpose(1, 2, 3, 0, 4).reshape(27, channels, channels)
    run = paired_rows if lax.axis_size("height") == 2 else single_rows
    decoded, summed, partial = run(
        frames,
        cache_in,
        taps_kernel,
        conv_bias.reshape(1, channels),
        cotangent.reshape(-1, channels),
    )
    kernel_grad = summed.reshape(3, 3, 3, -1, channels).transpose(3, 0, 1, 2, 4)
    partial = partial.reshape(4, rows, columns, channels)
    cache_grad = partial[:2].astype(jnp.bfloat16)
    carried = shifted(cache_grad, "tm", -1)
    frame_grad = (partial[2:] + carried.astype(jnp.float32)).astype(jnp.bfloat16)
    return decoded.reshape(frames.shape), frame_grad, cache_grad, kernel_grad


def solution(mesh):
    split = P("tm", "height", "width", None)
    in_specs = (split, P(None, "height", "width", None), P(), P(), split)
    out_specs = (split, split, split, P("height", None, None, None, None))
    return jax.shard_map(body, mesh=mesh, in_specs=in_specs, out_specs=out_specs, check_vma=False)
```

```python
import functools

import jax
import jax.numpy as jnp
from jax import lax
from jax.experimental import pallas as pl
from jax.experimental.pallas import tpu as pltpu
from jax.sharding import PartitionSpec as P

VMEM_LIMIT = 48 * 1024 * 1024
CHUNKS = 3


def shifted(value, axis, by):
    length = lax.axis_size(axis)
    pairs = [(i, i + by) for i in range(length) if 0 <= i + by < length]
    return lax.ppermute(value, axis, pairs)


def with_halo(value, axis, dim):
    length = value.shape[dim]
    before = shifted(lax.slice_in_dim(value, length - 1, length, axis=dim), axis, 1)
    after = shifted(lax.slice_in_dim(value, 0, 1, axis=dim), axis, -1)
    return jnp.concatenate([before, value, after], axis=dim)


def column_taps(padded, columns):
    return jnp.stack([padded[:, :, c : c + columns] for c in range(3)], 0)


def full_spec(shape):
    return pl.BlockSpec(shape, lambda *_: (0,) * len(shape), pipeline_mode=pl.Buffered(1))


def first_row(paired, rows):
    return lax.axis_index("height") * rows if paired else 0


def forward_kernel(rows, paired, taps_ref, kernel_ref, bias_ref, cot_ref, dec_ref, sc_ref, acc):
    step = pl.program_id(0)
    tap_t, tap_h = step // 3, step % 3
    channels = acc.shape[1]
    start = first_row(paired, rows)
    total = None
    for c in range(3):
        block = taps_ref[c, pl.ds(tap_t, 2), pl.ds(start + tap_h, rows)].reshape(-1, channels)
        part = lax.dot_general(
            block, kernel_ref[c], (((1,), (1,)), ((), ())), preferred_element_type=jnp.float32
        )
        total = part if total is None else total + part

    @pl.when(step == 0)
    def _():
        acc[...] = total + bias_ref[...]

    @pl.when(step > 0)
    def _():
        acc[...] += total

    @pl.when(step == 8)
    def _():
        pre = acc[...]
        sigma = jax.nn.sigmoid(pre)
        dec_ref[...] = (pre * sigma).astype(jnp.bfloat16)
        cot = cot_ref[...].astype(jnp.float32)
        sc_ref[...] = (cot * sigma * (1.0 + pre * (1.0 - sigma))).astype(jnp.bfloat16)


def forward(taps, kernel, bias, cotangent, rows, paired):
    _, _, _, columns, channels = taps.shape
    count = 2 * rows * columns
    flat = jax.ShapeDtypeStruct((count, channels), jnp.bfloat16)
    return pl.pallas_call(
        functools.partial(forward_kernel, rows, paired),
        grid=(9,),
        in_specs=[
            full_spec(taps.shape),
            pl.BlockSpec((3, channels, channels), lambda s: (s, 0, 0)),
            full_spec((1, channels)),
            full_spec((count, channels)),
        ],
        out_specs=[full_spec((count, channels))] * 2,
        out_shape=[flat, flat],
        scratch_shapes=[pltpu.VMEM((count, channels), jnp.float32)],
        compiler_params=pltpu.CompilerParams(vmem_limit_bytes=VMEM_LIMIT),
        cost_estimate=pl.CostEstimate(
            flops=54 * count * channels * channels,
            bytes_accessed=54 * channels * channels,
            transcendentals=count * channels,
        ),
        name="conv_forward",
    )(taps, kernel, bias, cotangent)


def data_kernel(rows, columns, paired, taps_ref, kernel_ref, part_ref):
    step = pl.program_id(0)
    tap_t, tap_h = step // 3, step % 3
    count, channels = rows * columns, part_ref.shape[-1]
    start = first_row(paired, rows)
    total = None
    for c in range(3):
        block = taps_ref[2 - c, :, pl.ds(start + 2 - tap_h, rows)].reshape(-1, channels)
        part = jnp.dot(block, kernel_ref[c], preferred_element_type=jnp.float32)
        total = part if total is None else total + part

    @pl.when(step == 0)
    def _():
        part_ref[...] = jnp.zeros_like(part_ref)

    part_ref[pl.ds(tap_t, 2)] += total.reshape(2, count, channels)


def data_grad(taps, kernel, rows, paired):
    _, _, _, columns, channels = taps.shape
    shape = (4, rows * columns, channels)
    return pl.pallas_call(
        functools.partial(data_kernel, rows, columns, paired),
        grid=(9,),
        in_specs=[
            full_spec(taps.shape),
            pl.BlockSpec((3, channels, channels), lambda s: (s, 0, 0)),
        ],
        out_specs=full_spec(shape),
        out_shape=jax.ShapeDtypeStruct(shape, jnp.float32),
        compiler_params=pltpu.CompilerParams(vmem_limit_bytes=VMEM_LIMIT),
        cost_estimate=pl.CostEstimate(
            flops=108 * rows * columns * channels * channels,
            bytes_accessed=54 * channels * channels,
            transcendentals=0,
        ),
        name="conv_data_grad",
    )(taps, kernel)


def weight_kernel(rows, taps_ref, scaled_ref, out_ref):
    step = pl.program_id(0)
    tap_t, tap_h = step // 3, step % 3
    channels = out_ref.shape[-1]
    for c in range(3):
        block = taps_ref[c, pl.ds(tap_t, 2), pl.ds(tap_h, rows)].reshape(-1, channels)
        part = jnp.dot(scaled_ref[...], block, preferred_element_type=jnp.float32)
        out_ref[c] = part.astype(out_ref.dtype)


def weight_grad(taps, scaled_t):
    _, _, rows, columns, channels = taps.shape
    rows -= 2
    owned = scaled_t.shape[0]
    return pl.pallas_call(
        functools.partial(weight_kernel, rows),
        grid=(9,),
        in_specs=[full_spec(taps.shape), full_spec(scaled_t.shape)],
        out_specs=pl.BlockSpec((3, owned, channels), lambda s: (s, 0, 0)),
        out_shape=jax.ShapeDtypeStruct((28, owned, channels), jnp.bfloat16),
        compiler_params=pltpu.CompilerParams(vmem_limit_bytes=VMEM_LIMIT),
        cost_estimate=pl.CostEstimate(
            flops=108 * rows * columns * owned * channels,
            bytes_accessed=54 * owned * channels,
            transcendentals=0,
        ),
        name="conv_weight_grad",
    )(taps, scaled_t)


def exchange_kernel(depth, *refs):
    sources, edges = refs[:depth], refs[depth : 2 * depth]
    main_ref, edge_ref, send_sem, recv_sem = refs[2 * depth :]
    mesh_id = pl.DeviceIdType.MESH
    k, h, w = (lax.axis_index(axis) for axis in ("tm", "height", "width"))
    times, widths = lax.axis_size("tm"), lax.axis_size("width")
    left, right = lax.rem(w + widths - 1, widths), lax.rem(w + 1, widths)

    barrier = pltpu.get_barrier_semaphore()
    count = 0
    for slot in range(2 * depth):
        dk, dh = slot // 2, slot % 2
        sender = lax.rem(k + times - dk, times), (1 - h if dh else h)
        for column in (left, right) + ((w,) if slot else ()):
            pl.semaphore_signal(
                barrier, inc=1, device_id=sender + (column,), device_id_type=mesh_id
            )
            count += 1
    pl.semaphore_wait(barrier, count)

    copies = []
    for slot in range(2 * depth):
        dk, dh = slot // 2, slot % 2
        target = lax.rem(k + dk, times), (1 - h if dh else h)
        plan = [(edges[dk].at[0], edge_ref.at[slot, 0], left)]
        plan.append((edges[dk].at[1], edge_ref.at[slot, 1], right))
        if slot:
            plan.append((sources[dk], main_ref.at[slot - 1], w))
        for source, place, column in plan:
            index = len(copies)
            copy = pltpu.make_async_remote_copy(
                src_ref=source,
                dst_ref=place,
                send_sem=send_sem.at[index],
                recv_sem=recv_sem.at[index],
                device_id=target + (column,),
                device_id_type=mesh_id,
            )
            copy.start()
            copies.append(copy)
    for copy in copies:
        copy.wait()


def exchange(sources, collective_id):
    depth = len(sources)
    shape = sources[0].shape
    channels = shape[-1]
    rim = shape[0] * shape[1]
    padded = -(-rim // 16) * 16

    def columns_of(value):
        ends = jnp.stack([value[:, :, 0], value[:, :, -1]], 0).reshape(2, rim, channels)
        return jnp.pad(ends, ((0, 0), (0, padded - rim), (0, 0)))

    edges = [columns_of(value) for value in sources]
    copies = 6 * depth - 1
    vmem = pl.BlockSpec(memory_space=pltpu.VMEM)
    main, ends = pl.pallas_call(
        functools.partial(exchange_kernel, depth),
        in_specs=[vmem] * (2 * depth),
        out_specs=[vmem] * 2,
        out_shape=[
            jax.ShapeDtypeStruct((2 * depth - 1,) + shape, jnp.bfloat16),
            jax.ShapeDtypeStruct((2 * depth, 2, padded, channels), jnp.bfloat16),
        ],
        scratch_shapes=[pltpu.SemaphoreType.DMA((copies,)), pltpu.SemaphoreType.DMA((copies,))],
        compiler_params=pltpu.CompilerParams(collective_id=collective_id, has_side_effects=True),
        name="exchange_%d" % depth,
    )(*sources, *edges)
    ends = ends[:, :, :rim].reshape(2 * depth, 2, shape[0], shape[1], 1, channels)
    return main, ends


def join_rows(mine, other, ends_mine, ends_other):
    place, column = lax.axis_index("height"), lax.axis_index("width")
    last = lax.axis_size("width") - 1

    def wide(value, ends):
        before = jnp.where(column == 0, jnp.zeros_like(ends[1]), ends[1])
        after = jnp.where(column == last, jnp.zeros_like(ends[0]), ends[0])
        return jnp.concatenate([before, value, after], 2)

    mine, other = wide(mine, ends_mine), wide(other, ends_other)
    edge = jnp.zeros_like(mine[:, :1])
    return jnp.where(
        place == 0,
        jnp.concatenate([edge, mine, other, edge], 1),
        jnp.concatenate([edge, other, mine, edge], 1),
    )


def sum_kernel(widths, in_ref, whole, got1, sent2, got2, sent3, got3, send_sem, recv_sem):
    size = in_ref.shape[0] // CHUNKS
    half, quarter = size // 2, size // 4
    piece = quarter // widths
    mesh_id = pl.DeviceIdType.MESH
    k, h, w = (lax.axis_index(axis) for axis in ("tm", "height", "width"))
    core, chip = lax.rem(k, 2), k // 2
    core_mate = (k + 1 - 2 * core, h, w)
    chip_mate = (lax.rem(k + 2, 4), h, w)
    line = [(k, h, lax.rem(w + d, widths)) for d in range(1, widths)]
    f32, bf16 = jnp.float32, jnp.bfloat16

    barrier = pltpu.get_barrier_semaphore()
    for mate in [core_mate, chip_mate] + line:
        pl.semaphore_signal(barrier, inc=1, device_id=mate, device_id_type=mesh_id)
    pl.semaphore_wait(barrier, 1 + widths)

    def rows(start, count):
        return pl.ds(pl.multiple_of(start, 16), count)

    used = []

    def send(source, place, mate):
        index = len(used)
        used.append(index)
        copy = pltpu.make_async_remote_copy(
            src_ref=source,
            dst_ref=place,
            send_sem=send_sem.at[index],
            recv_sem=recv_sem.at[index],
            device_id=mate,
            device_id_type=mesh_id,
        )
        copy.start()
        return copy

    base = [c * size for c in range(CHUNKS)]
    own_half = [b + core * half for b in base]
    own_quarter = [b + chip * quarter for b in own_half]
    own_piece = [b + w * piece for b in own_quarter]

    first = [
        send(in_ref.at[rows(base[c] + (1 - core) * half, half)], got1.at[c], core_mate)
        for c in range(CHUNKS)
    ]
    second, third, fourth, fifth, sixth = [], [], [], [], []
    for c in range(CHUNKS):
        first[c].wait()
        away = (1 - chip) * quarter
        mine = in_ref[rows(own_half[c] + away, quarter)].astype(f32)
        sent2[c] = (mine + got1[c, rows(away, quarter)].astype(f32)).astype(bf16)
        second.append(send(sent2.at[c], got2.at[c], chip_mate))
    for c in range(CHUNKS):
        second[c].wait()
        mine = in_ref[rows(own_quarter[c], quarter)].astype(f32)
        mine = mine + got1[c, rows(chip * quarter, quarter)].astype(f32)
        sent3[c] = (mine + got2[c].astype(f32)).astype(bf16)
        third.append(
            [
                send(sent3.at[c, rows(mate[2] * piece, piece)], got3.at[c, d], mate)
                for d, mate in enumerate(line)
            ]
        )
    for c in range(CHUNKS):
        total = in_ref[rows(own_piece[c], piece)].astype(f32)
        total = total + got1[c, rows(chip * quarter + w * piece, piece)].astype(f32)
        total = total + got2[c, rows(w * piece, piece)].astype(f32)
        for d, copy in enumerate(third[c]):
            copy.wait()
            total = total + got3[c, d].astype(f32)
        whole[rows(own_piece[c], piece)] = total.astype(bf16)
        place = whole.at[rows(own_piece[c], piece)]
        fourth.append([send(place, place, mate) for mate in line])
    for c in range(CHUNKS):
        for copy in fourth[c]:
            copy.wait()
        place = whole.at[rows(own_quarter[c], quarter)]
        fifth.append(send(place, place, chip_mate))
    for c in range(CHUNKS):
        fifth[c].wait()
        place = whole.at[rows(own_half[c], half)]
        sixth.append(send(place, place, core_mate))
    for c in range(CHUNKS):
        sixth[c].wait()


def sum_blocks(local, valid):
    total, channels = local.shape
    widths = lax.axis_size("width")
    size = total // CHUNKS
    half, quarter = size // 2, size // 4
    copies = CHUNKS * (4 + 2 * (widths - 1))
    bf16 = jnp.bfloat16
    vmem = pl.BlockSpec(memory_space=pltpu.VMEM)
    summed = pl.pallas_call(
        functools.partial(sum_kernel, widths),
        in_specs=[vmem],
        out_specs=vmem,
        out_shape=jax.ShapeDtypeStruct((total, channels), bf16),
        scratch_shapes=[
            pltpu.VMEM((CHUNKS, half, channels), bf16),
            pltpu.VMEM((CHUNKS, quarter, channels), bf16),
            pltpu.VMEM((CHUNKS, quarter, channels), bf16),
            pltpu.VMEM((CHUNKS, quarter, channels), bf16),
            pltpu.VMEM((CHUNKS, widths - 1, quarter // widths, channels), bf16),
            pltpu.SemaphoreType.DMA((copies,)),
            pltpu.SemaphoreType.DMA((copies,)),
        ],
        compiler_params=pltpu.CompilerParams(
            collective_id=2, has_side_effects=True, vmem_limit_bytes=VMEM_LIMIT
        ),
        name="sum_blocks",
    )(local)
    return summed[:valid].astype(jnp.float32)


def reduce_weights(owned):
    return lax.psum(owned, ("tm", "width")).astype(jnp.float32)


def paired_rows(frames, cache_in, kernel, bias, cotangent):
    rows, columns, channels = frames.shape[1:]
    place = lax.axis_index("height")
    is_last = lax.axis_index("tm") == lax.axis_size("tm") - 1
    onward = jnp.where(is_last, cache_in, frames)
    main, ends = exchange([frames, onward], 0)
    both = join_rows(
        jnp.concatenate([main[1], frames], 0),
        jnp.concatenate([main[2], main[0]], 0),
        jnp.concatenate([ends[2], ends[0]], 1),
        jnp.concatenate([ends[3], ends[1]], 1),
    )
    taps = column_taps(both, columns)
    decoded, scaled = forward(taps, kernel, bias, cotangent, rows, True)

    mine = scaled.reshape(frames.shape)
    main, ends = exchange([mine], 1)
    other = main[0]
    half = channels // 2
    upper, lower = jnp.where(place == 0, mine, other), jnp.where(place == 0, other, mine)
    joint = jnp.concatenate([upper, lower], 1).reshape(-1, channels)
    joint = jnp.where(place == 0, joint[:, :half], joint[:, half:])
    local = weight_grad(taps, joint.T)
    unit = 16 * 4 * lax.axis_size("width") * CHUNKS
    if lax.axis_size("tm") == 4 and 28 * half % unit == 0:
        summed = sum_blocks(local.reshape(28 * half, channels), 27 * half)
    else:
        summed = reduce_weights(local[:27])
    grad_taps = column_taps(join_rows(mine, other, ends[0], ends[1]), columns)
    return decoded, summed, data_grad(grad_taps, kernel, rows, True)


def single_rows(frames, cache_in, kernel, bias, cotangent):
    rows, columns, _ = frames.shape[1:]
    earlier = shifted(frames, "tm", 1)
    earlier = jnp.where(lax.axis_index("tm") == 0, cache_in, earlier)
    stacked = jnp.concatenate([earlier, frames], 0)
    taps = column_taps(with_halo(with_halo(stacked, "height", 1), "width", 2), columns)
    decoded, scaled = forward(taps, kernel, bias, cotangent, rows, False)
    owned = lax.psum_scatter(
        weight_grad(taps, scaled.T)[:27], "height", scatter_dimension=1, tiled=True
    )
    scaled4 = scaled.reshape(frames.shape)
    grad_taps = column_taps(with_halo(with_halo(scaled4, "height", 1), "width", 2), columns)
    return decoded, reduce_weights(owned), data_grad(grad_taps, kernel, rows, False)


def body(frames, cache_in, kernel, conv_bias, cotangent):
    _, rows, columns, channels = frames.shape
    taps_kernel = kernel.transpose(1, 2, 3, 0, 4).reshape(27, channels, channels)
    run = paired_rows if lax.axis_size("height") == 2 else single_rows
    decoded, summed, partial = run(
        frames,
        cache_in,
        taps_kernel,
        conv_bias.reshape(1, channels),
        cotangent.reshape(-1, channels),
    )
    kernel_grad = summed.reshape(3, 3, 3, -1, channels).transpose(3, 0, 1, 2, 4)
    partial = partial.reshape(4, rows, columns, channels)
    cache_grad = partial[:2].astype(jnp.bfloat16)
    carried = shifted(cache_grad, "tm", -1)
    frame_grad = (partial[2:] + carried.astype(jnp.float32)).astype(jnp.bfloat16)
    return decoded.reshape(frames.shape), frame_grad, cache_grad, kernel_grad


def solution(mesh):
    split = P("tm", "height", "width", None)
    in_specs = (split, P(None, "height", "width", None), P(), P(), split)
    out_specs = (split, split, split, P("height", None, None, None, None))
    return jax.shard_map(body, mesh=mesh, in_specs=in_specs, out_specs=out_specs, check_vma=False)
```
